32 devices in a mesh: groups: 2 (over x), mult: 16 (over z, y, core).
Axes of the slice: x: 2, y: 2, z: 4, core: 2. Of those that a mesh axis runs over, the one named last changes fastest.
Arguments:
- wavefunction: bfloat16 [4096, 256], P(('groups', 'mult')), parts along dimension 0, may hold values from -6 to 6
- multiplet_spins: int32 [2048], P(('groups', 'mult')), parts along dimension 0, may hold values from 0 to 6
- left_tiles: bfloat16 [7168, 128, 128], P(('groups', 'mult')), parts along dimension 0, may hold values from -0.046875 to 0.046875
- task_info: int32 [7168, 2], P(('groups', 'mult')), parts along dimension 0, may hold values from -4 to 37, as said below
- task_count: int32 [32], P(('groups', 'mult')), parts along dimension 0, may hold values from 28 to 224, as said below
- right_ops: bfloat16 [76, 256, 256], P('groups'), parts along dimension 0, may hold values from -0.375 to 0.375
Outputs:
- applied: float32 [4096, 256], P(('groups', 'mult')), parts along dimension 0
The draws below stay inside these ranges and needn't reach their ends.
There are 2 independent parts, one for each index of `groups`. The reference program is written for one: setup_inputs(seed, part) draws one part's arguments, and reference() takes and returns one part's arrays. A program takes and returns all parts, laid end to end along the dimension named above; each array names one. Nothing has to cross between parts.
Inputs may be any that keep to these rules, and one draw needn't show every extreme that they name: `task_info`: column 0 is the offset from a task's output block to its input block; the input block lies within 4 blocks and inside 0 to 15. Column 1 is the MPO bond index, below 38. `task_count`: at least one block has all 224 slots live.
All inputs are finite; a program needn't handle non-finite values.
Results may differ from the reference program's by a relative error of at most 0.005.
Values may be sent and summed in bfloat16 or wider, within the bound.
A program may use at most 64 MiB of HBM per device.

```python
import jax
import jax.numpy as jnp
from jax import lax

MULT_DEV = 64
W = 38
RCOL = 256
TASK_DEV = 224
BAND = 4
ROWS = 128
BLOCKS = 16
MULTS = 1024
ROWS_ALL = 2048
TASKS = 3584


def draw_task_info(key, part):
    key = jax.random.fold_in(key, 11)
    first_key, second_key = jax.random.split(key)
    slot_block = jnp.arange(TASKS, dtype=jnp.int32) // TASK_DEV
    lowest = jnp.maximum(-BAND, -slot_block)
    highest = jnp.minimum(BAND, BLOCKS - 1 - slot_block)
    offsets = jax.random.randint(first_key, (TASKS,), lowest, highest + 1, dtype=jnp.int32)
    bond_ids = jax.random.randint(second_key, (TASKS,), 0, W, dtype=jnp.int32)
    return jnp.stack([offsets, bond_ids], axis=1)


def draw_task_count(key, part):
    key = jax.random.fold_in(key, 23)
    first_key, second_key = jax.random.split(key)
    ranking = jax.random.permutation(first_key, BLOCKS)
    heavy_block = ranking < max(1, BLOCKS // 8)
    light_count = jax.random.randint(second_key, (BLOCKS,), TASK_DEV // 8, TASK_DEV // 2 + 1, dtype=jnp.int32)
    return jnp.where(heavy_block, TASK_DEV, light_count).astype(jnp.int32)


def with_ends(entries, rng, low, top_value):
    longest = entries.shape.index(max(entries.shape))
    spots = []
    for shift in (0, 1):
        where = [jax.random.randint(jax.random.fold_in(rng, axis), (), 0, length) for axis, length in enumerate(entries.shape)]
        where[longest] = (where[longest] + shift) % entries.shape[longest]
        spots.append(tuple(where))
    return entries.at[spots[0]].set(low).at[spots[1]].set(top_value)


def levels(own_key, shape, cuts, smallest, high):
    level = 1.0
    for position, blocks in cuts:
        steps = jax.random.uniform(jax.random.fold_in(jax.random.fold_in(own_key, 6), position), (blocks,), jnp.float32, smallest / len(cuts), high / len(cuts))
        level = level * jnp.repeat(jnp.exp(steps), shape[position] // blocks).reshape((-1,) + (1,) * (len(shape) - 1 - position))
    return level


def centred(stream_key, shape, width, most, cuts=(), kind=jnp.bfloat16):
    values = width * jax.random.normal(stream_key, shape, jnp.float32)
    if cuts:
        values = values * levels(stream_key, shape, cuts, -0.22, 0.18)
    return jnp.clip(values, -most, most).astype(kind)


def setup_inputs(seed: int = 0, part: int = 0) -> dict:
    key_list = jax.random.split(jax.random.key(seed), 7)
    part_splits = jax.random.split(jax.random.fold_in(key_list[6], part), 7)
    wavefunction = centred(part_splits[0], (ROWS_ALL, RCOL), 1.0, 6.0, ((0, 16),))
    multiplet_spins = with_ends(jax.random.randint(part_splits[1], (MULTS,), 0, 7), jax.random.fold_in(part_splits[1], 1), 0, 6).astype(jnp.int32)
    left_tiles = centred(part_splits[2], (TASKS, ROWS, ROWS), (ROWS * TASK_DEV // 2) ** -0.5, 0.046875, ((0, 16),))
    task_info = draw_task_info(jax.random.fold_in(jax.random.fold_in(key_list[6], part), 71), part)
    task_count = draw_task_count(jax.random.fold_in(jax.random.fold_in(key_list[6], part), 71), part)
    right_ops = centred(part_splits[5], (W, RCOL, RCOL), RCOL ** -0.5, 0.375)
    return dict(wavefunction=wavefunction, multiplet_spins=multiplet_spins, left_tiles=left_tiles, task_info=task_info, task_count=task_count, right_ops=right_ops)


def reference(wavefunction, multiplet_spins, left_tiles, task_info, task_count, right_ops):
    block_rows = 2 * MULT_DEV
    roots = jnp.repeat(jnp.sqrt((2 * multiplet_spins + 1).astype(jnp.float32)), 2)
    source = (wavefunction.astype(jnp.float32) * roots[:, None]).astype(jnp.bfloat16)
    blocks = source.reshape(BLOCKS, block_rows, RCOL)
    padding = jnp.zeros((BAND, block_rows, RCOL), jnp.bfloat16)
    padded = jnp.concatenate([padding, blocks, padding], axis=0)
    tiles_all = left_tiles.reshape(BLOCKS, TASK_DEV, block_rows, block_rows)
    info_all = task_info.reshape(BLOCKS, TASK_DEV, 2)
    right_wide = right_ops.astype(jnp.float32)

    def one_block(inputs):
        block_index, block_tiles, block_info, live_count = inputs
        window = lax.dynamic_slice_in_dim(padded, block_index, 2 * BAND + 1, 0)
        picked = jnp.take(window, block_info[:, 0] + BAND, axis=0)
        product = jnp.einsum('tij,tjc->tic', block_tiles.astype(jnp.float32), picked.astype(jnp.float32), precision=lax.Precision.HIGHEST).astype(jnp.bfloat16)
        living = jnp.arange(TASK_DEV, dtype=jnp.int32) < live_count
        selector = ((block_info[:, 1][:, None] == jnp.arange(W, dtype=jnp.int32)[None, :]) & living[:, None]).astype(jnp.float32)
        summed = jnp.einsum('ta,tic->aic', selector, product.astype(jnp.float32), precision=lax.Precision.HIGHEST)
        return jnp.einsum('aic,acq->iq', summed, right_wide, precision=lax.Precision.HIGHEST)
    indices = jnp.arange(BLOCKS, dtype=jnp.int32)
    result = lax.map(one_block, (indices, tiles_all, info_all, task_count))
    return result.reshape(BLOCKS * block_rows, RCOL) / roots[:, None]
```

```python
import functools

import jax
import jax.numpy as jnp
from jax import lax
from jax.experimental import pallas as pl
from jax.experimental.pallas import tpu as pltpu
from jax.sharding import PartitionSpec as P

BAND = 4
GROUP = 16
DISTANCES = tuple(d for k in range(1, BAND + 1) for d in (k, -k))


def in_range(index, total):
    return jnp.logical_and(index >= 0, index < total)


def row_roots(spins, rows):
    mults = spins.shape[1]
    row = lax.broadcasted_iota(jnp.int32, (rows, mults), 0) >> 1
    col = lax.broadcasted_iota(jnp.int32, (rows, mults), 1)
    dims = jnp.where(row == col, 2 * spins + 1, 0).astype(jnp.float32)
    return jnp.sqrt(jnp.sum(dims, axis=1, keepdims=True))


def kernel(
    mult,
    count_ref,
    info_ref,
    spins_ref,
    wave_ref,
    tiles_hbm,
    right_hbm,
    out_ref,
    ext,
    tiles,
    right,
    stacked,
    send_sem,
    recv_sem,
    tile_sem,
    right_sem,
):
    me = lax.axis_index("mult")
    rows = wave_ref.shape[0]
    slots = tiles.shape[0]
    barrier = pltpu.get_barrier_semaphore()
    for d in DISTANCES:
        @pl.when(in_range(me + d, mult))
        def _():
            pl.semaphore_signal(
                barrier,
                inc=1,
                device_id={"mult": me + d},
                device_id_type=pl.DeviceIdType.MESH,
            )

    right_copy = pltpu.make_async_copy(right_hbm, right, right_sem)
    right_copy.start()
    tile_copies = []
    for g in range(slots // GROUP):
        part = pl.ds(g * GROUP, GROUP)
        copy = pltpu.make_async_copy(tiles_hbm.at[part], tiles.at[part], tile_sem.at[g])
        copy.start()

    roots = row_roots(spins_ref[...], rows)
    ext[BAND] = (wave_ref[...].astype(jnp.float32) * roots).astype(jnp.bfloat16)
    ext[2 * BAND + 1] = jnp.zeros_like(wave_ref)
    out_ref[...] = jnp.zeros_like(out_ref)

    neighbours = sum(in_range(me + d, mult).astype(jnp.int32) for d in DISTANCES)
    pl.semaphore_wait(barrier, neighbours)
    copies = []
    for k, d in enumerate(DISTANCES):
        copy = pltpu.make_async_remote_copy(
            src_ref=ext.at[BAND],
            dst_ref=ext.at[BAND - d],
            send_sem=send_sem.at[k],
            recv_sem=recv_sem.at[k],
            device_id={"mult": me + d},
            device_id_type=pl.DeviceIdType.MESH,
        )
        copies.append(copy)
        pl.when(in_range(me + d, mult))(copy.start)
    for d, copy in zip(DISTANCES, copies):
        pl.when(in_range(me - d, mult))(copy.wait_recv)
    right_copy.wait()
    live = count_ref[0]

    def add_group(g, carry):
        first = g * GROUP
        part = pl.ds(first, GROUP)
        pltpu.make_async_copy(tiles_hbm.at[part], tiles.at[part], tile_sem.at[g]).wait()
        lefts = []
        for j in range(GROUP):
            t = first + j
            block = jnp.where(t < live, info_ref[0, t] + BAND, 2 * BAND + 1)
            bond = info_ref[1, t]
            term = jnp.dot(ext[block], right[bond], preferred_element_type=jnp.float32)
            stacked[pl.ds(j * rows, rows), :] = term.astype(jnp.bfloat16)
            lefts.append(tiles[t])
        out_ref[...] += jnp.dot(
            jnp.concatenate(lefts, axis=1), stacked[...], preferred_element_type=jnp.float32
        )
        return carry

    lax.fori_loop(0, slots // GROUP, add_group, 0)
    out_ref[...] = out_ref[...] / roots
    for d, copy in zip(DISTANCES, copies):
        pl.when(in_range(me + d, mult))(copy.wait_send)


def body(mult, wavefunction, multiplet_spins, left_tiles, task_info, task_count, right_ops):
    rows, columns = wavefunction.shape
    slots = left_tiles.shape[0]
    vmem = pl.BlockSpec(memory_space=pltpu.VMEM)
    smem = pl.BlockSpec(memory_space=pltpu.SMEM)
    hbm = pl.BlockSpec(memory_space=pl.ANY)
    return pl.pallas_call(
        functools.partial(kernel, mult),
        out_shape=jax.ShapeDtypeStruct((rows, columns), jnp.float32),
        in_specs=[smem, smem, vmem, vmem, hbm, hbm],
        out_specs=vmem,
        scratch_shapes=[
            pltpu.VMEM((2 * BAND + 2, rows, columns), jnp.bfloat16),
            pltpu.VMEM(left_tiles.shape, jnp.bfloat16),
            pltpu.VMEM(right_ops.shape, jnp.bfloat16),
            pltpu.VMEM((GROUP * rows, columns), jnp.bfloat16),
            pltpu.SemaphoreType.DMA((len(DISTANCES),)),
            pltpu.SemaphoreType.DMA((len(DISTANCES),)),
            pltpu.SemaphoreType.DMA((slots // GROUP,)),
            pltpu.SemaphoreType.DMA,
        ],
        compiler_params=pltpu.CompilerParams(
            collective_id=0, has_side_effects=True, vmem_limit_bytes=60 * 1024 * 1024
        ),
    )(
        task_count,
        task_info.T,
        multiplet_spins.reshape(1, -1),
        wavefunction,
        left_tiles,
        right_ops,
    )


def solution(mesh):
    placed = (
        P(("groups", "mult"), None),
        P(("groups", "mult")),
        P(("groups", "mult"), None, None),
        P(("groups", "mult"), None),
        P(("groups", "mult")),
        P("groups", None, None),
    )
    return jax.shard_map(
        functools.partial(body, mesh.shape["mult"]),
        mesh=mesh,
        in_specs=placed,
        out_specs=P(("groups", "mult"), None),
        check_vma=False,
    )
```

```python
import functools

import jax
import jax.numpy as jnp
from jax import lax
from jax.experimental import pallas as pl
from jax.experimental.pallas import tpu as pltpu
from jax.sharding import PartitionSpec as P

BAND = 4
GROUP = 32
UNROLL = 4
ZERO_BLOCK = 2 * BAND + 1
HOPS = tuple(d for k in range(2, BAND + 1, 2) for d in (k, -k))


def in_range(index, total):
    return jnp.logical_and(index >= 0, index < total)


def row_roots(spins, rows):
    mults = spins.shape[1]
    row = lax.broadcasted_iota(jnp.int32, (rows, mults), 0) >> 1
    col = lax.broadcasted_iota(jnp.int32, (rows, mults), 1)
    dims = jnp.where(row == col, 2 * spins + 1, 0).astype(jnp.float32)
    return jnp.sqrt(jnp.sum(dims, axis=1, keepdims=True))


def total(condition, values, axis):
    return jnp.sum(jnp.where(condition, values, 0), axis=axis, keepdims=True)


def bond_plan(info, live, bonds, pairs, width):
    slots = info.shape[1]

    def grid(shape, axis):
        return lax.broadcasted_iota(jnp.int32, shape, axis)

    square = (slots, slots)
    slot_down, slot_along = grid(square, 0), grid(square, 1)
    bond_along = jnp.where(grid((1, slots), 1) < live, info[1:2], bonds)
    bond_down = total(slot_down == slot_along, bond_along, 1)
    block_down = total(slot_down == slot_along, info[0:1] + BAND, 1)
    earlier = (bond_down == bond_along) & (slot_along < slot_down)
    rank = total(earlier, 1, 1)

    small = (bonds, bonds)
    low, high = grid(small, 0), grid(small, 1)
    counts = total(grid((bonds, slots), 0) == bond_along, 1, 1)
    half = (counts + 1) >> 1
    half_along = total(low == high, half, 0)
    start = total(high < low, half_along, 1)
    start_along = total(low == high, start, 0)
    base = total(grid((slots, bonds), 1) == bond_down, start_along, 1)
    position = jnp.where(bond_down < bonds, 2 * base + rank, -1)

    marks = grid((slots, width), 0) + (block_down << 16) + (1 << 24)
    order = total(position == grid((slots, width), 1), marks, 0)
    order = jnp.where(order == 0, ZERO_BLOCK << 16, order & ((1 << 24) - 1))
    opens = total((start == grid((bonds, width), 1)) & (counts > 0), 1, 0)
    carries = jnp.where(opens > 0, 0, 1)
    last = jnp.where(counts > 0, start + half - 1, pairs)
    last = total(grid((bonds, width), 0) == grid((bonds, width), 1), last, 0)
    row = grid((8, width), 0)
    return jnp.where(row == 0, order, jnp.where(row == 1, carries, last))


def kernel(
    mult,
    count_ref,
    info_ref,
    spins_ref,
    wave_ref,
    tiles_hbm,
    right_hbm,
    out_ref,
    ext,
    tiles,
    right,
    sums,
    plan_vmem,
    plan,
    send_sem,
    recv_sem,
    pass_sem,
    got_sem,
    tile_sem,
    right_sem,
    plan_sem,
):
    me = lax.axis_index("mult")
    partner = me + 1 - 2 * lax.rem(me, 2)
    is_even = lax.rem(me, 2) == 0
    rows = wave_ref.shape[0]
    slots = tiles.shape[0]
    bonds = right.shape[0]
    pairs = sums.shape[0] - 1
    mesh_id = pl.DeviceIdType.MESH
    barrier = pltpu.get_barrier_semaphore()
    for d in HOPS:
        @pl.when(in_range(me + d, mult))
        def _():
            pl.semaphore_signal(
                barrier, inc=1, device_id={"mult": me + d}, device_id_type=mesh_id
            )
    pl.semaphore_signal(barrier, inc=1, device_id={"mult": partner}, device_id_type=mesh_id)

    roots = row_roots(spins_ref[...], rows)
    ext[BAND] = (wave_ref[...].astype(jnp.float32) * roots).astype(jnp.bfloat16)

    neighbours = sum(in_range(me + d, mult).astype(jnp.int32) for d in HOPS) + 1
    pl.semaphore_wait(barrier, neighbours)
    hops = []
    for k, d in enumerate(HOPS):
        copy = pltpu.make_async_remote_copy(
            src_ref=ext.at[BAND],
            dst_ref=ext.at[BAND - d],
            send_sem=send_sem.at[k],
            recv_sem=recv_sem.at[k],
            device_id={"mult": me + d},
            device_id_type=mesh_id,
        )
        hops.append(copy)
        pl.when(in_range(me + d, mult))(copy.start)

    def hand_over(k, offset):
        to_odd = pltpu.make_async_remote_copy(
            src_ref=ext.at[BAND + offset],
            dst_ref=ext.at[max(BAND + offset - 1, 0)],
            send_sem=pass_sem.at[k],
            recv_sem=got_sem.at[k],
            device_id={"mult": partner},
            device_id_type=mesh_id,
        )
        to_even = pltpu.make_async_remote_copy(
            src_ref=ext.at[BAND + offset],
            dst_ref=ext.at[min(BAND + offset + 1, 2 * BAND)],
            send_sem=pass_sem.at[k],
            recv_sem=got_sem.at[k],
            device_id={"mult": partner},
            device_id_type=mesh_id,
        )
        return to_odd, to_even

    def sends(offset):
        exists = in_range(me + offset, mult)
        odd_wants = jnp.logical_and(exists, is_even) if offset > -BAND else None
        even_wants = jnp.logical_and(exists, jnp.logical_not(is_even)) if offset < BAND else None
        return odd_wants, even_wants

    def gets(offset):
        exists = in_range(partner + offset, mult)
        from_odd = jnp.logical_and(exists, is_even) if offset < BAND else None
        from_even = jnp.logical_and(exists, jnp.logical_not(is_even)) if offset > -BAND else None
        return from_odd, from_even

    passes = [(0, 0)] + [(k + 1, -d) for k, d in enumerate(HOPS)]
    handed = [hand_over(k, offset) for k, offset in passes]

    def when_either(conditions, actions):
        for condition, action in zip(conditions, actions):
            if condition is not None:
                pl.when(condition)(action)

    when_either(sends(0), [c.start for c in handed[0]])

    right_copy = pltpu.make_async_copy(right_hbm, right, right_sem)
    tile_copies = []
    for g in range(slots // GROUP):
        part = pl.ds(g * GROUP, GROUP)
        copy = pltpu.make_async_copy(tiles_hbm.at[part], tiles.at[part], tile_sem.at[g])
        copy.start()
        tile_copies.append(copy)
    right_copy.start()

    ext[ZERO_BLOCK] = jnp.zeros_like(wave_ref)
    sums[pairs] = jnp.zeros_like(wave_ref)
    plan_vmem[...] = bond_plan(info_ref[...], count_ref[0], bonds, pairs, plan_vmem.shape[1])
    plan_copy = pltpu.make_async_copy(plan_vmem, plan, plan_sem)
    plan_copy.start()

    for (k, offset), both, copy, d in zip(passes[1:], handed[1:], hops, HOPS):
        pl.when(in_range(me - d, mult))(copy.wait_recv)
        when_either(sends(offset), [c.start for c in both])
    plan_copy.wait()
    for copy in tile_copies:
        copy.wait()
    for (k, offset), both in zip(passes, handed):
        when_either(gets(offset), [c.wait_recv for c in both])

    def add_pair(p, run):
        first, second = plan[0, 2 * p], plan[0, 2 * p + 1]
        left = jnp.concatenate([tiles[first & 0xFFFF], tiles[second & 0xFFFF]], axis=1)
        source = jnp.concatenate([ext[first >> 16], ext[second >> 16]], axis=0)
        run = jnp.where(plan[1, p] > 0, run, 0.0) + jnp.dot(
            left, source, preferred_element_type=jnp.float32
        )
        sums[p] = run.astype(jnp.bfloat16)
        return run

    lax.fori_loop(0, pairs, add_pair, jnp.zeros(out_ref.shape, jnp.float32), unroll=UNROLL)
    right_copy.wait()
    lefts = [sums[plan[2, a]] for a in range(bonds)]
    out_ref[...] = (
        jnp.dot(
            jnp.concatenate(lefts, axis=1),
            right[...].reshape(bonds * right.shape[1], right.shape[2]),
            preferred_element_type=jnp.float32,
        )
        / roots
    )
    for d, copy in zip(HOPS, hops):
        pl.when(in_range(me + d, mult))(copy.wait_send)
    for (k, offset), both in zip(passes, handed):
        when_either(sends(offset), [c.wait_send for c in both])


def body(mult, wavefunction, multiplet_spins, left_tiles, task_info, task_count, right_ops):
    rows, columns = wavefunction.shape
    slots = left_tiles.shape[0]
    bonds = right_ops.shape[0]
    pairs = -(-((slots + bonds) // 2) // UNROLL) * UNROLL
    width = -(-max(2 * pairs, bonds) // 128) * 128
    vmem = pl.BlockSpec(memory_space=pltpu.VMEM)
    smem = pl.BlockSpec(memory_space=pltpu.SMEM)
    hbm = pl.BlockSpec(memory_space=pl.ANY)
    return pl.pallas_call(
        functools.partial(kernel, mult),
        out_shape=jax.ShapeDtypeStruct((rows, columns), jnp.float32),
        in_specs=[smem, vmem, vmem, vmem, hbm, hbm],
        out_specs=vmem,
        scratch_shapes=[
            pltpu.VMEM((2 * BAND + 2, rows, columns), jnp.bfloat16),
            pltpu.VMEM(left_tiles.shape, jnp.bfloat16),
            pltpu.VMEM(right_ops.shape, jnp.bfloat16),
            pltpu.VMEM((pairs + 1, rows, columns), jnp.bfloat16),
            pltpu.VMEM((8, width), jnp.int32),
            pltpu.SMEM((8, width), jnp.int32),
            pltpu.SemaphoreType.DMA((len(HOPS),)),
            pltpu.SemaphoreType.DMA((len(HOPS),)),
            pltpu.SemaphoreType.DMA((len(HOPS) + 1,)),
            pltpu.SemaphoreType.DMA((len(HOPS) + 1,)),
            pltpu.SemaphoreType.DMA((slots // GROUP,)),
            pltpu.SemaphoreType.DMA,
            pltpu.SemaphoreType.DMA,
        ],
        compiler_params=pltpu.CompilerParams(
            collective_id=0, has_side_effects=True, vmem_limit_bytes=60 * 1024 * 1024
        ),
    )(
        task_count,
        task_info.T,
        multiplet_spins.reshape(1, -1),
        wavefunction,
        left_tiles,
        right_ops,
    )


def solution(mesh):
    placed = (
        P(("groups", "mult"), None),
        P(("groups", "mult")),
        P(("groups", "mult"), None, None),
        P(("groups", "mult"), None),
        P(("groups", "mult")),
        P("groups", None, None),
    )
    return jax.shard_map(
        functools.partial(body, mesh.shape["mult"]),
        mesh=mesh,
        in_specs=placed,
        out_specs=P(("groups", "mult"), None),
        check_vma=False,
    )
```

```python
import functools

import jax
import jax.numpy as jnp
from jax import lax
from jax.experimental import pallas as pl
from jax.experimental.pallas import tpu as pltpu
from jax.sharding import PartitionSpec as P

BAND = 4
GROUP = 32
UNROLL = 66
ZERO_BLOCK = 2 * BAND + 1
HOPS = tuple(d for k in range(2, BAND + 1, 2) for d in (k, -k))


def in_range(index, total):
    return jnp.logical_and(index >= 0, index < total)


def row_roots(spins, rows):
    mults = spins.shape[1]
    row = lax.broadcasted_iota(jnp.int32, (rows, mults), 0) >> 1
    col = lax.broadcasted_iota(jnp.int32, (rows, mults), 1)
    dims = jnp.where(row == col, 2 * spins + 1, 0).astype(jnp.float32)
    return jnp.sqrt(jnp.sum(dims, axis=1, keepdims=True))


def total(condition, values, axis):
    return jnp.sum(jnp.where(condition, values, 0), axis=axis, keepdims=True)


def bond_plan(info, live, bonds, pairs, width):
    slots = info.shape[1]

    def grid(shape, axis):
        return lax.broadcasted_iota(jnp.int32, shape, axis)

    square = (slots, slots)
    slot_down, slot_along = grid(square, 0), grid(square, 1)
    bond_along = jnp.where(grid((1, slots), 1) < live, info[1:2], bonds)
    bond_down = total(slot_down == slot_along, bond_along, 1)
    block_down = total(slot_down == slot_along, info[0:1] + BAND, 1)
    earlier = (bond_down == bond_along) & (slot_along < slot_down)
    rank = total(earlier, 1, 1)

    small = (bonds, bonds)
    low, high = grid(small, 0), grid(small, 1)
    counts = total(grid((bonds, slots), 0) == bond_along, 1, 1)
    half = (counts + 1) >> 1
    half_along = total(low == high, half, 0)
    start = total(high < low, half_along, 1)
    start_along = total(low == high, start, 0)
    base = total(grid((slots, bonds), 1) == bond_down, start_along, 1)
    position = jnp.where(bond_down < bonds, 2 * base + rank, -1)

    marks = grid((slots, width), 0) + (block_down << 16) + (1 << 24)
    order = total(position == grid((slots, width), 1), marks, 0)
    order = jnp.where(order == 0, ZERO_BLOCK << 16, order & ((1 << 24) - 1))
    opens = total((start == grid((bonds, width), 1)) & (counts > 0), 1, 0)
    carries = jnp.where(opens > 0, 0, 1)
    last = jnp.where(counts > 0, start + half - 1, pairs)
    last = total(grid((bonds, width), 0) == grid((bonds, width), 1), last, 0)
    row = grid((8, width), 0)
    return jnp.where(row == 0, order, jnp.where(row == 1, carries, last))


def kernel(
    mult,
    count_hbm,
    info_hbm,
    spins_hbm,
    wave_hbm,
    tiles_hbm,
    right_hbm,
    out_ref,
    count_ref,
    info_ref,
    spins_ref,
    wave_ref,
    ext,
    tiles,
    right,
    sums,
    plan_vmem,
    plan,
    send_sem,
    recv_sem,
    pass_sem,
    got_sem,
    tile_sem,
    right_sem,
    plan_sem,
    small_sem,
):
    me = lax.axis_index("mult")
    partner = me + 1 - 2 * lax.rem(me, 2)
    is_even = lax.rem(me, 2) == 0
    rows = wave_ref.shape[0]
    slots = tiles.shape[0]
    bonds = right.shape[0]
    pairs = sums.shape[0] - 1
    mesh_id = pl.DeviceIdType.MESH
    barrier = pltpu.get_barrier_semaphore()
    for d in HOPS:
        @pl.when(in_range(me + d, mult))
        def _():
            pl.semaphore_signal(
                barrier, inc=1, device_id={"mult": me + d}, device_id_type=mesh_id
            )
    pl.semaphore_signal(barrier, inc=1, device_id={"mult": partner}, device_id_type=mesh_id)

    small_copies = [
        pltpu.make_async_copy(source, target, small_sem.at[i])
        for i, (source, target) in enumerate(
            [(spins_hbm, spins_ref), (wave_hbm, wave_ref), (info_hbm, info_ref), (count_hbm, count_ref)]
        )
    ]
    for copy in small_copies:
        copy.start()
    ext[ZERO_BLOCK] = jnp.zeros_like(wave_ref)
    sums[pairs] = jnp.zeros_like(wave_ref)
    for copy in small_copies:
        copy.wait()
    roots = row_roots(spins_ref[...], rows)
    ext[BAND] = (wave_ref[...].astype(jnp.float32) * roots).astype(jnp.bfloat16)

    neighbours = sum(in_range(me + d, mult).astype(jnp.int32) for d in HOPS) + 1
    pl.semaphore_wait(barrier, neighbours)
    hops = []
    for k, d in enumerate(HOPS):
        copy = pltpu.make_async_remote_copy(
            src_ref=ext.at[BAND],
            dst_ref=ext.at[BAND - d],
            send_sem=send_sem.at[k],
            recv_sem=recv_sem.at[k],
            device_id={"mult": me + d},
            device_id_type=mesh_id,
        )
        hops.append(copy)
        pl.when(in_range(me + d, mult))(copy.start)

    def hand_over(k, offset):
        to_odd = pltpu.make_async_remote_copy(
            src_ref=ext.at[BAND + offset],
            dst_ref=ext.at[max(BAND + offset - 1, 0)],
            send_sem=pass_sem.at[k],
            recv_sem=got_sem.at[k],
            device_id={"mult": partner},
            device_id_type=mesh_id,
        )
        to_even = pltpu.make_async_remote_copy(
            src_ref=ext.at[BAND + offset],
            dst_ref=ext.at[min(BAND + offset + 1, 2 * BAND)],
            send_sem=pass_sem.at[k],
            recv_sem=got_sem.at[k],
            device_id={"mult": partner},
            device_id_type=mesh_id,
        )
        return to_odd, to_even

    def sends(offset):
        exists = in_range(me + offset, mult)
        odd_wants = jnp.logical_and(exists, is_even) if offset > -BAND else None
        even_wants = jnp.logical_and(exists, jnp.logical_not(is_even)) if offset < BAND else None
        return odd_wants, even_wants

    def gets(offset):
        exists = in_range(partner + offset, mult)
        from_odd = jnp.logical_and(exists, is_even) if offset < BAND else None
        from_even = jnp.logical_and(exists, jnp.logical_not(is_even)) if offset > -BAND else None
        return from_odd, from_even

    passes = [(0, 0)] + [(k + 1, -d) for k, d in enumerate(HOPS)]
    handed = [hand_over(k, offset) for k, offset in passes]

    def when_either(conditions, actions):
        for condition, action in zip(conditions, actions):
            if condition is not None:
                pl.when(condition)(action)

    when_either(sends(0), [c.start for c in handed[0]])

    right_copy = pltpu.make_async_copy(right_hbm, right, right_sem)
    tile_copies = []
    for g in range(slots // GROUP):
        part = pl.ds(g * GROUP, GROUP)
        copy = pltpu.make_async_copy(tiles_hbm.at[part], tiles.at[part], tile_sem.at[g])
        copy.start()
        tile_copies.append(copy)
    right_copy.start()
    plan_vmem[...] = bond_plan(info_ref[...], count_ref[0], bonds, pairs, plan_vmem.shape[1])
    plan_copy = pltpu.make_async_copy(plan_vmem, plan, plan_sem)
    plan_copy.start()

    for (k, offset), both, copy, d in zip(passes[1:], handed[1:], hops, HOPS):
        pl.when(in_range(me - d, mult))(copy.wait_recv)
        when_either(sends(offset), [c.start for c in both])
    plan_copy.wait()
    for copy in tile_copies:
        copy.wait()
    for (k, offset), both in zip(passes, handed):
        when_either(gets(offset), [c.wait_recv for c in both])

    def add_pair(p, run):
        first, second = plan[0, 2 * p], plan[0, 2 * p + 1]
        left = jnp.concatenate([tiles[first & 0xFFFF], tiles[second & 0xFFFF]], axis=1)
        source = jnp.concatenate([ext[first >> 16], ext[second >> 16]], axis=0)
        run = jnp.where(plan[1, p] > 0, run, 0.0) + jnp.dot(
            left, source, preferred_element_type=jnp.float32
        )
        sums[p] = run.astype(jnp.bfloat16)
        return run

    lax.fori_loop(0, pairs, add_pair, jnp.zeros(out_ref.shape, jnp.float32), unroll=UNROLL)
    right_copy.wait()
    lefts = [sums[plan[2, a]] for a in range(bonds)]
    out_ref[...] = (
        jnp.dot(
            jnp.concatenate(lefts, axis=1),
            right[...].reshape(bonds * right.shape[1], right.shape[2]),
            preferred_element_type=jnp.float32,
        )
        / roots
    )
    for d, copy in zip(HOPS, hops):
        pl.when(in_range(me + d, mult))(copy.wait_send)
    for (k, offset), both in zip(passes, handed):
        when_either(sends(offset), [c.wait_send for c in both])


def body(mult, wavefunction, multiplet_spins, left_tiles, task_info, task_count, right_ops):
    rows, columns = wavefunction.shape
    slots = left_tiles.shape[0]
    bonds = right_ops.shape[0]
    pairs = -(-((slots + bonds) // 2) // UNROLL) * UNROLL
    width = -(-max(2 * pairs, bonds) // 128) * 128
    vmem = pl.BlockSpec(memory_space=pltpu.VMEM)
    hbm = pl.BlockSpec(memory_space=pl.ANY)
    return pl.pallas_call(
        functools.partial(kernel, mult),
        out_shape=jax.ShapeDtypeStruct((rows, columns), jnp.float32),
        in_specs=[hbm] * 6,
        out_specs=vmem,
        scratch_shapes=[
            pltpu.SMEM((1,), jnp.int32),
            pltpu.VMEM((2, slots), jnp.int32),
            pltpu.VMEM((1, rows // 2), jnp.int32),
            pltpu.VMEM((rows, columns), jnp.bfloat16),
            pltpu.VMEM((2 * BAND + 2, rows, columns), jnp.bfloat16),
            pltpu.VMEM(left_tiles.shape, jnp.bfloat16),
            pltpu.VMEM(right_ops.shape, jnp.bfloat16),
            pltpu.VMEM((pairs + 1, rows, columns), jnp.bfloat16),
            pltpu.VMEM((8, width), jnp.int32),
            pltpu.SMEM((8, width), jnp.int32),
            pltpu.SemaphoreType.DMA((len(HOPS),)),
            pltpu.SemaphoreType.DMA((len(HOPS),)),
            pltpu.SemaphoreType.DMA((len(HOPS) + 1,)),
            pltpu.SemaphoreType.DMA((len(HOPS) + 1,)),
            pltpu.SemaphoreType.DMA((slots // GROUP,)),
            pltpu.SemaphoreType.DMA,
            pltpu.SemaphoreType.DMA,
            pltpu.SemaphoreType.DMA((4,)),
        ],
        compiler_params=pltpu.CompilerParams(
            collective_id=0, has_side_effects=True, vmem_limit_bytes=60 * 1024 * 1024
        ),
    )(
        task_count,
        task_info.T,
        multiplet_spins.reshape(1, -1),
        wavefunction,
        left_tiles,
        right_ops,
    )


def solution(mesh):
    placed = (
        P(("groups", "mult"), None),
        P(("groups", "mult")),
        P(("groups", "mult"), None, None),
        P(("groups", "mult"), None),
        P(("groups", "mult")),
        P("groups", None, None),
    )
    return jax.shard_map(
        functools.partial(body, mesh.shape["mult"]),
        mesh=mesh,
        in_specs=placed,
        out_specs=P(("groups", "mult"), None),
        check_vma=False,
    )
```

```python
import functools

import jax
import jax.numpy as jnp
from jax import lax
from jax.experimental import pallas as pl
from jax.experimental.pallas import tpu as pltpu
from jax.sharding import PartitionSpec as P

BAND = 4
GROUP = 32
UNROLL = 66
ZERO_BLOCK = 2 * BAND + 1
HOPS = tuple(d for k in range(BAND, 1, -2) for d in (k, -k))


def in_range(index, total):
    return jnp.logical_and(index >= 0, index < total)


def row_roots(spins, rows):
    mults = spins.shape[1]
    row = lax.broadcasted_iota(jnp.int32, (rows, mults), 0) >> 1
    col = lax.broadcasted_iota(jnp.int32, (rows, mults), 1)
    dims = jnp.where(row == col, 2 * spins + 1, 0).astype(jnp.float32)
    return jnp.sqrt(jnp.sum(dims, axis=1, keepdims=True))


def total(condition, values, axis):
    return jnp.sum(jnp.where(condition, values, 0), axis=axis, keepdims=True)


def bond_plan(info, live, bonds, pairs, width):
    slots = info.shape[1]

    def grid(shape, axis):
        return lax.broadcasted_iota(jnp.int32, shape, axis)

    square = (slots, slots)
    slot_down, slot_along = grid(square, 0), grid(square, 1)
    bond_along = jnp.where(grid((1, slots), 1) < live, info[1:2], bonds)
    bond_down = total(slot_down == slot_along, bond_along, 1)
    block_down = total(slot_down == slot_along, info[0:1] + BAND, 1)
    earlier = (bond_down == bond_along) & (slot_along < slot_down)
    rank = total(earlier, 1, 1)

    small = (bonds, bonds)
    low, high = grid(small, 0), grid(small, 1)
    counts = total(grid((bonds, slots), 0) == bond_along, 1, 1)
    half = (counts + 1) >> 1
    half_along = total(low == high, half, 0)
    start = total(high < low, half_along, 1)
    start_along = total(low == high, start, 0)
    base = total(grid((slots, bonds), 1) == bond_down, start_along, 1)
    position = jnp.where(bond_down < bonds, 2 * base + rank, -1)

    marks = grid((slots, width), 0) + (block_down << 16) + (1 << 24)
    order = total(position == grid((slots, width), 1), marks, 0)
    order = jnp.where(order == 0, ZERO_BLOCK << 16, order & ((1 << 24) - 1))
    opens = total((start == grid((bonds, width), 1)) & (counts > 0), 1, 0)
    carries = jnp.where(opens > 0, 0, 1)
    last = jnp.where(counts > 0, start + half - 1, pairs)
    last = total(grid((bonds, width), 0) == grid((bonds, width), 1), last, 0)
    row = grid((8, width), 0)
    return jnp.where(row == 0, order, jnp.where(row == 1, carries, last))


def kernel(
    mult,
    count_hbm,
    info_hbm,
    spins_hbm,
    wave_hbm,
    tiles_hbm,
    right_hbm,
    out_ref,
    count_ref,
    info_ref,
    spins_ref,
    wave_ref,
    ext,
    tiles,
    right,
    sums,
    plan_vmem,
    plan,
    send_sem,
    recv_sem,
    pass_sem,
    got_sem,
    tile_sem,
    right_sem,
    plan_sem,
    small_sem,
):
    me = lax.axis_index("mult")
    partner = me + 1 - 2 * lax.rem(me, 2)
    is_even = lax.rem(me, 2) == 0
    rows = wave_ref.shape[0]
    slots = tiles.shape[0]
    bonds = right.shape[0]
    pairs = sums.shape[0] - 1
    mesh_id = pl.DeviceIdType.MESH
    barrier = pltpu.get_barrier_semaphore()
    for d in HOPS:
        @pl.when(in_range(me + d, mult))
        def _():
            pl.semaphore_signal(
                barrier, inc=1, device_id={"mult": me + d}, device_id_type=mesh_id
            )
    pl.semaphore_signal(barrier, inc=1, device_id={"mult": partner}, device_id_type=mesh_id)

    small_copies = [
        pltpu.make_async_copy(source, target, small_sem.at[i])
        for i, (source, target) in enumerate(
            [(spins_hbm, spins_ref), (wave_hbm, wave_ref), (info_hbm, info_ref), (count_hbm, count_ref)]
        )
    ]
    for copy in small_copies:
        copy.start()
    ext[ZERO_BLOCK] = jnp.zeros_like(wave_ref)
    sums[pairs] = jnp.zeros_like(wave_ref)
    for copy in small_copies:
        copy.wait()
    roots = row_roots(spins_ref[...], rows)
    ext[BAND] = (wave_ref[...].astype(jnp.float32) * roots).astype(jnp.bfloat16)

    neighbours = sum(in_range(me + d, mult).astype(jnp.int32) for d in HOPS) + 1
    pl.semaphore_wait(barrier, neighbours)
    hops = []
    for k, d in enumerate(HOPS):
        copy = pltpu.make_async_remote_copy(
            src_ref=ext.at[BAND],
            dst_ref=ext.at[BAND - d],
            send_sem=send_sem.at[k],
            recv_sem=recv_sem.at[k],
            device_id={"mult": me + d},
            device_id_type=mesh_id,
        )
        hops.append(copy)
        pl.when(in_range(me + d, mult))(copy.start)

    def hand_over(k, offset):
        to_odd = pltpu.make_async_remote_copy(
            src_ref=ext.at[BAND + offset],
            dst_ref=ext.at[max(BAND + offset - 1, 0)],
            send_sem=pass_sem.at[k],
            recv_sem=got_sem.at[k],
            device_id={"mult": partner},
            device_id_type=mesh_id,
        )
        to_even = pltpu.make_async_remote_copy(
            src_ref=ext.at[BAND + offset],
            dst_ref=ext.at[min(BAND + offset + 1, 2 * BAND)],
            send_sem=pass_sem.at[k],
            recv_sem=got_sem.at[k],
            device_id={"mult": partner},
            device_id_type=mesh_id,
        )
        return to_odd, to_even

    def sends(offset):
        exists = in_range(me + offset, mult)
        odd_wants = jnp.logical_and(exists, is_even) if offset > -BAND else None
        even_wants = jnp.logical_and(exists, jnp.logical_not(is_even)) if offset < BAND else None
        return odd_wants, even_wants

    def gets(offset):
        exists = in_range(partner + offset, mult)
        from_odd = jnp.logical_and(exists, is_even) if offset < BAND else None
        from_even = jnp.logical_and(exists, jnp.logical_not(is_even)) if offset > -BAND else None
        return from_odd, from_even

    passes = [(0, 0)] + [(k + 1, -d) for k, d in enumerate(HOPS)]
    handed = [hand_over(k, offset) for k, offset in passes]

    def when_either(conditions, actions):
        for condition, action in zip(conditions, actions):
            if condition is not None:
                pl.when(condition)(action)

    when_either(sends(0), [c.start for c in handed[0]])

    right_copy = pltpu.make_async_copy(right_hbm, right, right_sem)
    tile_copies = []
    for g in range(slots // GROUP):
        part = pl.ds(g * GROUP, GROUP)
        copy = pltpu.make_async_copy(tiles_hbm.at[part], tiles.at[part], tile_sem.at[g])
        copy.start()
        tile_copies.append(copy)
    right_copy.start()
    plan_vmem[...] = bond_plan(info_ref[...], count_ref[0], bonds, pairs, plan_vmem.shape[1])
    plan_copy = pltpu.make_async_copy(plan_vmem, plan, plan_sem)
    plan_copy.start()

    for (k, offset), both, copy, d in zip(passes[1:], handed[1:], hops, HOPS):
        pl.when(in_range(me - d, mult))(copy.wait_recv)
        when_either(sends(offset), [c.start for c in both])
    plan_copy.wait()
    for copy in tile_copies:
        copy.wait()
    for (k, offset), both in zip(passes, handed):
        when_either(gets(offset), [c.wait_recv for c in both])

    def add_pair(p, run):
        first, second = plan[0, 2 * p], plan[0, 2 * p + 1]
        left = jnp.concatenate([tiles[first & 0xFFFF], tiles[second & 0xFFFF]], axis=1)
        source = jnp.concatenate([ext[first >> 16], ext[second >> 16]], axis=0)
        run = jnp.where(plan[1, p] > 0, run, 0.0) + jnp.dot(
            left, source, preferred_element_type=jnp.float32
        )
        sums[p] = run.astype(jnp.bfloat16)
        return run

    lax.fori_loop(0, pairs, add_pair, jnp.zeros(out_ref.shape, jnp.float32), unroll=UNROLL)
    right_copy.wait()
    lefts = [sums[plan[2, a]] for a in range(bonds)]
    out_ref[...] = (
        jnp.dot(
            jnp.concatenate(lefts, axis=1),
            right[...].reshape(bonds * right.shape[1], right.shape[2]),
            preferred_element_type=jnp.float32,
        )
        / roots
    )
    for d, copy in zip(HOPS, hops):
        pl.when(in_range(me + d, mult))(copy.wait_send)
    for (k, offset), both in zip(passes, handed):
        when_either(sends(offset), [c.wait_send for c in both])


def body(mult, wavefunction, multiplet_spins, left_tiles, task_info, task_count, right_ops):
    rows, columns = wavefunction.shape
    slots = left_tiles.shape[0]
    bonds = right_ops.shape[0]
    pairs = -(-((slots + bonds) // 2) // UNROLL) * UNROLL
    width = -(-max(2 * pairs, bonds) // 128) * 128
    vmem = pl.BlockSpec(memory_space=pltpu.VMEM)
    hbm = pl.BlockSpec(memory_space=pl.ANY)
    return pl.pallas_call(
        functools.partial(kernel, mult),
        out_shape=jax.ShapeDtypeStruct((rows, columns), jnp.float32),
        in_specs=[hbm] * 6,
        out_specs=vmem,
        scratch_shapes=[
            pltpu.SMEM((1,), jnp.int32),
            pltpu.VMEM((2, slots), jnp.int32),
            pltpu.VMEM((1, rows // 2), jnp.int32),
            pltpu.VMEM((rows, columns), jnp.bfloat16),
            pltpu.VMEM((2 * BAND + 2, rows, columns), jnp.bfloat16),
            pltpu.VMEM(left_tiles.shape, jnp.bfloat16),
            pltpu.VMEM(right_ops.shape, jnp.bfloat16),
            pltpu.VMEM((pairs + 1, rows, columns), jnp.bfloat16),
            pltpu.VMEM((8, width), jnp.int32),
            pltpu.SMEM((8, width), jnp.int32),
            pltpu.SemaphoreType.DMA((len(HOPS),)),
            pltpu.SemaphoreType.DMA((len(HOPS),)),
            pltpu.SemaphoreType.DMA((len(HOPS) + 1,)),
            pltpu.SemaphoreType.DMA((len(HOPS) + 1,)),
            pltpu.SemaphoreType.DMA((slots // GROUP,)),
            pltpu.SemaphoreType.DMA,
            pltpu.SemaphoreType.DMA,
            pltpu.SemaphoreType.DMA((4,)),
        ],
        compiler_params=pltpu.CompilerParams(
            collective_id=0, has_side_effects=True, vmem_limit_bytes=60 * 1024 * 1024
        ),
    )(
        task_count,
        task_info.T,
        multiplet_spins.reshape(1, -1),
        wavefunction,
        left_tiles,
        right_ops,
    )


def solution(mesh):
    placed = (
        P(("groups", "mult"), None),
        P(("groups", "mult")),
        P(("groups", "mult"), None, None),
        P(("groups", "mult"), None),
        P(("groups", "mult")),
        P("groups", None, None),
    )
    return jax.shard_map(
        functools.partial(body, mesh.shape["mult"]),
        mesh=mesh,
        in_specs=placed,
        out_specs=P(("groups", "mult"), None),
        check_vma=False,
    )
```
